32 devices in a mesh: row: 8 (over y, x, core), col: 4 (over z).
Axes of the slice: x: 2, y: 2, z: 4, core: 2. Of those that a mesh axis runs over, the one named last changes fastest.
Arguments:
- tokens: int32 [256], replicated, may hold values from 0 to 8191
- emission_table: bfloat16 [8192, 32768], P('row', 'col'), may hold values from -3 to 0
- forward_rows: bfloat16 [256, 32768], P('col', 'row'), may hold values from 0.05 to 64
- backward_rows: bfloat16 [256, 32768], P('row', 'col'), may hold values from 0.05 to 64
- src_embed: bfloat16 [32768, 256], P(('row', 'col')), may hold values from -12 to 12
- tgt_embed: bfloat16 [32768, 256], P(('col', 'row')), may hold values from -12 to 12
Outputs:
- grad_src: float32 [32768, 256], P(('row', 'col'))
- grad_tgt: float32 [32768, 256], P(('col', 'row'))
The draws below stay inside these ranges and needn't reach their ends.
All inputs are finite; a program needn't handle non-finite values.
Results may differ from the reference program's by a relative error of at most 0.018.
Values may be sent and summed in bfloat16 or wider, within the bound.
A program may use at most 384 MiB of HBM per device.

```python
import math
import jax
import jax.numpy as jnp
import numpy as np
from jax import lax

S = 32768
E = 256
VOCAB = 8192
SEQS = 256


def embed_pair(key):
    key_src, key_tgt, key_row, key_col = jax.random.split(key, 4)
    src = jnp.clip(0.35 * jax.random.normal(key_src, (S, E), jnp.float32), -2.1, 2.1)
    tgt = jnp.clip(0.35 * jax.random.normal(key_tgt, (S, E), jnp.float32), -2.1, 2.1)
    state_index = jnp.arange(S, dtype=jnp.float32)
    upper_part = (state_index >= float(S - S // 4)).astype(jnp.float32)
    lift_size = 2.0 / math.sqrt(E)
    tgt = tgt * (1.0 + 0.3 * upper_part)[:, None] + lift_size * upper_part[:, None]
    src_wave = 1.5 * jnp.cos(2.0 * math.pi * state_index / float(S // 8))
    src = src + lift_size * src_wave[:, None]
    stride = S // 8
    anchor_src = jnp.arange(8, dtype=jnp.int32) * stride + jax.random.randint(key_row, (8,), 0, stride)
    anchor_tgt = jnp.arange(8, dtype=jnp.int32) * stride + jax.random.randint(key_col, (8,), 0, stride - 1)
    tgt = tgt.at[anchor_tgt].set(tgt[anchor_tgt])
    src = src.at[anchor_src].set(src[anchor_src])
    tgt = tgt.at[anchor_tgt + 1].set(tgt[anchor_tgt + 1])
    return (src, tgt)


def rising_rows(key, row_low, row_high):
    key_base, key_row, key_state = jax.random.split(key, 3)
    base = jnp.exp(jax.random.uniform(key_base, (SEQS, S), jnp.float32, math.log(0.6), math.log(1.6)))
    rise = 1.0 + 2.0 * jnp.arange(S, dtype=jnp.float32) / S
    state_scale = jnp.exp(jax.random.uniform(key_state, (1, S), jnp.float32, math.log(0.2), math.log(5.0)))
    row_scale = jnp.exp(jax.random.uniform(key_row, (SEQS, 1), jnp.float32, math.log(row_low), math.log(row_high)))
    return base * rise[None, :] * state_scale * row_scale


def draw_forward_rows(key, part):
    key = jax.random.fold_in(key, 5)
    row_low, row_high = (1.0, 1.0)
    return rising_rows(key, row_low, row_high).astype(jnp.bfloat16)


def draw_backward_rows(key, part):
    key = jax.random.fold_in(key, 7)
    row_low, row_high = (1.0, 1.0)
    return rising_rows(key, row_low, row_high).astype(jnp.bfloat16)


def draw_src_embed(key, part):
    src, tgt = embed_pair(key)
    return src.astype(jnp.bfloat16)


def draw_tgt_embed(key, part):
    src, tgt = embed_pair(key)
    return tgt.astype(jnp.bfloat16)


def touch_ends(values, rng, low, largest):
    longest = values.shape.index(max(values.shape))
    spots = []
    for shift in (0, 1):
        where = [jax.random.randint(jax.random.fold_in(rng, axis), (), 0, length) for axis, length in enumerate(values.shape)]
        where[longest] = (where[longest] + shift) % values.shape[longest]
        spots.append(tuple(where))
    return values.at[spots[0]].set(low).at[spots[1]].set(largest)


def levels(stream_key, extent, shards, smallest, largest):
    level = 1.0
    for dim, parts in shards:
        heights = jax.random.uniform(jax.random.fold_in(jax.random.fold_in(stream_key, 6), dim), (parts,), jnp.float32, smallest / len(shards), largest / len(shards))
        level = level * jnp.repeat(jnp.exp(heights), extent[dim] // parts).reshape((-1,) + (1,) * (len(extent) - 1 - dim))
    return level


def cumulative_ranks(number_of, skew):
    loads = [(1 << 20) // math.isqrt(grade ** skew) + 1 for grade in range(1, number_of + 1)]
    scale = 1 + sum(loads) // (1 << 30)
    return np.cumsum(np.array([max(1, weight // scale) for weight in loads]))


def ranked_ids(key, dims, number_of, lean):
    grid = cumulative_ranks(number_of, lean)
    ticket = jax.random.randint(jax.random.fold_in(key, 1), dims, 0, int(grid[number_of - 1]))
    standing = jnp.searchsorted(jnp.asarray(grid, jnp.int32), ticket, side="right")
    return jax.random.permutation(jax.random.fold_in(key, 2), number_of)[standing].astype(jnp.int32)


def setup_inputs(seed: int = 0) -> dict:
    splits = jax.random.split(jax.random.key(seed), 7)
    tokens = touch_ends(ranked_ids(splits[0], (SEQS,), VOCAB, 2), jax.random.fold_in(splits[0], 3), 0, VOCAB - 1).astype(jnp.int32)
    emission_table = jnp.clip(-3.0 + 3.0 * jax.random.uniform(splits[1], (VOCAB, S), jnp.float32) ** levels(splits[1], (VOCAB, S), ((0, 8), (1, 4)), -0.2, 0.2), -3.0, 0.0).astype(jnp.bfloat16)
    forward_rows = draw_forward_rows(jax.random.fold_in(splits[6], 71), 0)
    backward_rows = draw_backward_rows(jax.random.fold_in(splits[6], 71), 0)
    src_embed = draw_src_embed(jax.random.fold_in(splits[6], 71), 0)
    tgt_embed = draw_tgt_embed(jax.random.fold_in(splits[6], 71), 0)
    return {"tokens": tokens, "emission_table": emission_table, "forward_rows": forward_rows, "backward_rows": backward_rows, "src_embed": src_embed, "tgt_embed": tgt_embed}


def exp_rows(src_rows, tgt_embed):
    logits = lax.dot_general(src_rows, tgt_embed, (((1,), (1,)), ((), ())), preferred_element_type=jnp.float32)
    row_peak = jnp.max(logits, axis=1)
    exp_full = jnp.exp(logits - row_peak[:, None])
    return jnp.sum(exp_full, axis=1), exp_full.astype(jnp.bfloat16)


def reference(tokens, emission_table, forward_rows, backward_rows, src_embed, tgt_embed):
    rows_size = min(512, S)
    num_blocks = S // rows_size
    looked = jnp.take(emission_table, tokens, axis=0).astype(jnp.float32)
    weighted = (jnp.exp(looked) * backward_rows.astype(jnp.float32)).astype(jnp.bfloat16)
    src_blocks = src_embed.reshape(num_blocks, rows_size, E)

    def first_pass(src_rows):
        row_sums, exp_block = exp_rows(src_rows, tgt_embed)
        reach = lax.dot_general(weighted, exp_block, (((1,), (1,)), ((), ())), preferred_element_type=jnp.float32)
        return row_sums, reach

    totals, reaches = lax.map(first_pass, src_blocks)
    forward_blocks = forward_rows.astype(jnp.float32).reshape(SEQS, num_blocks, rows_size).transpose(1, 0, 2)
    norm_terms = jnp.sum(forward_blocks * reaches / totals[:, None, :], axis=(0, 2))
    factor = jnp.float32(S) / jnp.float32(SEQS)

    def second_pass(acc_tgt, inputs):
        src_rows, forward_block, row_sums = inputs
        unused, exp_block = exp_rows(src_rows, tgt_embed)
        coeffs = (factor * forward_block / (norm_terms[:, None] * row_sums[None, :])).astype(jnp.bfloat16)
        summed = lax.dot_general(coeffs, weighted, (((0,), (0,)), ((), ())), preferred_element_type=jnp.float32)
        exp_wide = exp_block.astype(jnp.float32)
        counts = exp_wide * summed
        row_counts = jnp.sum(counts, axis=1)
        grad_logits = (counts - exp_wide * (row_counts / row_sums)[:, None]).astype(jnp.bfloat16)
        grad_rows = jnp.dot(grad_logits, tgt_embed, preferred_element_type=jnp.float32)
        acc_tgt = acc_tgt + lax.dot_general(grad_logits, src_rows, (((0,), (0,)), ((), ())), preferred_element_type=jnp.float32)
        return acc_tgt, grad_rows

    grad_tgt, grad_blocks = lax.scan(second_pass, jnp.zeros((S, E), jnp.float32), (src_blocks, forward_blocks, totals))
    return grad_blocks.reshape(S, E), grad_tgt
```

```python
import jax
import jax.numpy as jnp
from jax import lax
from jax.experimental import pallas as pl
from jax.experimental.pallas import tpu as pltpu
from jax.sharding import PartitionSpec as P

S = 32768
SEQS = 256
NT = (((1,), (1,)), ((), ()))
BF16 = jnp.bfloat16
F32 = jnp.float32


def fit(size, want):
    while size % want:
        want //= 2
    return want


def first_pass(src, tgt, weighted):
    rows, width = src.shape
    cols = tgt.shape[0]
    seqs = weighted.shape[0]
    tile = fit(rows, 256)
    chunk = fit(cols, 1024)
    tiles = rows // tile

    def body(src_ref, tgt_ref, w_ref, e_ref, reach_ref, sum_ref, peak_ref, s0, s1, p0, p1):
        step = pl.program_id(0)

        def run(new, old, new_peak, old_peak):
            peak = old_peak[...]

            def go(c, carry):
                best, total, reach = carry
                at = pl.ds(pl.multiple_of(c * chunk, chunk), chunk)
                logits = lax.dot_general(src_ref[...], tgt_ref[at, :], NT, preferred_element_type=F32)
                new[:, at] = logits
                best = jnp.maximum(best, jnp.max(logits, axis=1, keepdims=True))
                e = jnp.exp(old[:, at] - peak)
                total = total + jnp.sum(e, axis=1, keepdims=True)
                eb = e.astype(BF16)
                e_ref[:, at] = eb
                reach = reach + lax.dot_general(eb, w_ref[:, at], NT, preferred_element_type=F32)
                return best, total, reach

            best, total, reach = lax.fori_loop(
                0,
                cols // chunk,
                go,
                (jnp.full((tile, 1), -jnp.inf, F32), jnp.zeros((tile, 1), F32), jnp.zeros((tile, seqs), F32)),
            )
            new_peak[...] = best
            reach_ref[...] = reach
            sum_ref[...] = total
            peak_ref[...] = peak

        @pl.when(lax.rem(step, 2) == 0)
        def _():
            run(s0, s1, p0, p1)

        @pl.when(lax.rem(step, 2) == 1)
        def _():
            run(s1, s0, p1, p0)

    ahead = lambda t: (jnp.minimum(t, tiles - 1), 0)
    behind = lambda t: (jnp.maximum(t - 1, 0), 0)
    whole = lambda t: (0, 0)
    return pl.pallas_call(
        body,
        grid=(tiles + 1,),
        in_specs=[
            pl.BlockSpec((tile, width), ahead),
            pl.BlockSpec((cols, width), whole),
            pl.BlockSpec((seqs, cols), whole),
        ],
        out_specs=[
            pl.BlockSpec((tile, cols), behind),
            pl.BlockSpec((tile, seqs), behind),
            pl.BlockSpec((tile, 1), behind),
            pl.BlockSpec((tile, 1), behind),
        ],
        out_shape=[
            jax.ShapeDtypeStruct((rows, cols), BF16),
            jax.ShapeDtypeStruct((rows, seqs), F32),
            jax.ShapeDtypeStruct((rows, 1), F32),
            jax.ShapeDtypeStruct((rows, 1), F32),
        ],
        scratch_shapes=[
            pltpu.VMEM((tile, cols), F32),
            pltpu.VMEM((tile, cols), F32),
            pltpu.VMEM((tile, 1), F32),
            pltpu.VMEM((tile, 1), F32),
        ],
        compiler_params=pltpu.CompilerParams(
            dimension_semantics=("arbitrary",), vmem_limit_bytes=58 * 1024 * 1024
        ),
        cost_estimate=pl.CostEstimate(
            flops=2 * rows * cols * (width + seqs), bytes_accessed=2 * rows * cols, transcendentals=rows * cols
        ),
        name="first_pass",
    )(src, tgt, weighted)


def second_pass(exp_block, coeffs, share, weighted, tgt, src, src_t):
    rows, cols = exp_block.shape
    width = tgt.shape[1]
    seqs = weighted.shape[0]
    tile = fit(rows, 512)
    chunk = fit(cols, 512)
    group = 4 if (cols // chunk) % 4 == 0 else 1

    def body(e_ref, c_ref, share_ref, w_ref, tgt_ref, st_ref, gs_ref, gt_ref):
        first = pl.program_id(0) == 0

        @pl.when(first)
        def _():
            gt_ref[...] = jnp.zeros_like(gt_ref)

        def go(c, total):
            for k in range(group):
                at = pl.ds(pl.multiple_of((c * group + k) * chunk, chunk), chunk)
                summed = jnp.dot(c_ref[...], w_ref[:, at], preferred_element_type=F32)
                g = (e_ref[:, at].astype(F32) * (summed - share_ref[...])).astype(BF16)
                total = total + jnp.dot(g, tgt_ref[at, :], preferred_element_type=F32)
                gt_ref[:, at] += jnp.dot(st_ref[...], g, preferred_element_type=F32)
            return total

        gs_ref[...] = lax.fori_loop(0, cols // chunk // group, go, jnp.zeros((tile, width), F32))

    by_row = lambda t: (t, 0)
    whole = lambda t: (0, 0)
    return pl.pallas_call(
        body,
        grid=(rows // tile,),
        in_specs=[
            pl.BlockSpec((tile, cols), by_row),
            pl.BlockSpec((tile, seqs), by_row),
            pl.BlockSpec((tile, 1), by_row),
            pl.BlockSpec((seqs, cols), whole, pipeline_mode=pl.Buffered(1)),
            pl.BlockSpec((cols, width), whole, pipeline_mode=pl.Buffered(1)),
            pl.BlockSpec((width, tile), lambda t: (0, t)),
        ],
        out_specs=[
            pl.BlockSpec((tile, width), by_row),
            pl.BlockSpec((width, cols), whole, pipeline_mode=pl.Buffered(1)),
        ],
        out_shape=[
            jax.ShapeDtypeStruct((rows, width), F32),
            jax.ShapeDtypeStruct((width, cols), F32),
        ],
        compiler_params=pltpu.CompilerParams(
            dimension_semantics=("arbitrary",), vmem_limit_bytes=58 * 1024 * 1024
        ),
        cost_estimate=pl.CostEstimate(
            flops=2 * rows * cols * (2 * width + seqs), bytes_accessed=2 * rows * cols, transcendentals=0
        ),
        name="second_pass",
    )(exp_block, coeffs, share, weighted, tgt, src_t)


def on_device(tokens, emission_table, forward_rows, backward_rows, src_embed, tgt_embed):
    src_block = lax.all_gather(src_embed, "col", axis=0, tiled=True)
    tgt_block = lax.all_gather(tgt_embed, "row", axis=0, tiled=True)
    vocab_local = emission_table.shape[0]
    offset = lax.axis_index("row") * vocab_local
    onehot = (tokens[:, None] == offset + jnp.arange(vocab_local, dtype=jnp.int32)[None, :]).astype(BF16)
    looked = jnp.dot(onehot, emission_table, preferred_element_type=F32).astype(BF16)
    mine = lax.psum_scatter(looked, "row", scatter_dimension=0, tiled=True).astype(F32)
    weighted = (jnp.exp(mine) * backward_rows.astype(F32)).astype(BF16)
    weighted = lax.all_gather(weighted, "row", axis=0, tiled=True)
    forward_all = lax.all_gather(forward_rows.T, "col", axis=1, tiled=True).astype(F32)

    exp_block, reach, local_sums, local_peak = first_pass(src_block, tgt_block, weighted)

    row_peak = lax.pmax(local_peak, "col")
    scale = jnp.exp(local_peak - row_peak)
    row_sums = lax.psum(local_sums * scale, "col")
    reach = reach * scale
    norm_terms = lax.psum(jnp.sum(forward_all * reach / row_sums, axis=0, keepdims=True), ("row", "col"))
    factor = F32(S) / F32(SEQS)
    coeffs = (factor * forward_all / (norm_terms * row_sums)).astype(BF16)
    row_counts = lax.psum(jnp.sum(coeffs.astype(F32) * reach, axis=1, keepdims=True), "col")
    share = row_counts / row_sums * scale
    coeffs = (coeffs.astype(F32) * scale).astype(BF16)

    part_src, part_tgt = second_pass(
        exp_block, coeffs, share, weighted, tgt_block, src_block, src_block.T
    )
    grad_src = lax.psum_scatter(part_src, "col", scatter_dimension=0, tiled=True)
    grad_tgt = lax.psum_scatter(part_tgt, "row", scatter_dimension=1, tiled=True).T
    return (grad_src, grad_tgt)


def solution(mesh):
    in_specs = (
        P(),
        P("row", "col"),
        P("col", "row"),
        P("row", "col"),
        P(("row", "col"), None),
        P(("col", "row"), None),
    )
    out_specs = (P(("row", "col"), None), P(("col", "row"), None))
    return jax.shard_map(
        on_device, mesh=mesh, in_specs=in_specs, out_specs=out_specs, check_vma=False
    )
```

```python
import functools

import jax
import jax.numpy as jnp
from jax import lax
from jax.experimental import pallas as pl
from jax.experimental.pallas import tpu as pltpu
from jax.sharding import PartitionSpec as P

NT = (((1,), (1,)), ((), ()))
BF16 = jnp.bfloat16
F32 = jnp.float32
MESH = pl.DeviceIdType.MESH
MIB = 1024 * 1024


def fit(size, want):
    while size % want:
        want //= 2
    return want


def to_row(column):
    return jnp.broadcast_to(column, (column.shape[0], 128)).T[:1]


def to_column(row):
    return jnp.broadcast_to(row, (128, row.shape[1])).T[:, :1]


def remote(src, dst, send, recv, device):
    return pltpu.make_async_remote_copy(
        src_ref=src, dst_ref=dst, send_sem=send, recv_sem=recv, device_id=device, device_id_type=MESH
    )


def greet(devices):
    barrier = pltpu.get_barrier_semaphore()
    for device in devices:
        pl.semaphore_signal(barrier, inc=1, device_id=device, device_id_type=MESH)
    pl.semaphore_wait(barrier, len(devices))


def row_peers(nrow):
    row, col = lax.axis_index("row"), lax.axis_index("col")
    half, pair, pairs = lax.rem(row, 2), row // 2, nrow // 2
    sibling = (pair * 2 + 1 - half, col)
    across = [(lax.rem(pair + d, pairs) * 2 + half, col) for d in range(1, pairs)]
    return row, half, pair, sibling, across


def gather_body(nrow, looked, back, tgt, tgt_all, w_all, pair_in, chip_in, own_w, *sems):
    (s1, r1, s2, r2, ts, tr, fs, fr, ws, wr, gs, gr, here) = sems
    pairs = nrow // 2
    row, half, pair, sibling, across = row_peers(nrow)
    greet([sibling] + across)

    first = [remote(looked.at[2 * q + 1 - half], pair_in.at[q], s1.at[q], r1.at[q], sibling) for q in range(pairs)]
    for copy in first:
        copy.start()
    keep = pltpu.make_async_copy(tgt, tgt_all.at[row], here.at[0])
    keep.start()
    tgt_out = [remote(tgt, tgt_all.at[row], ts.at[d], tr.at[d], to) for d, to in enumerate([sibling] + across)]
    for copy in tgt_out:
        copy.start()
    for copy in first:
        copy.wait()
    for q in range(pairs):
        pair_in[q] = (looked[2 * q + half].astype(F32) + pair_in[q].astype(F32)).astype(BF16)
    second = [
        remote(pair_in.at[lax.rem(pair + d, pairs)], chip_in.at[d], s2.at[d], r2.at[d], across[d - 1])
        for d in range(1, pairs)
    ]
    for copy in second:
        copy.start()
    for copy in second:
        copy.wait()
    looks = pair_in[pair].astype(F32)
    for d in range(1, pairs):
        looks = looks + chip_in[d].astype(F32)
    own_w[...] = (jnp.exp(looks) * back[...].astype(F32)).astype(BF16)
    keep_w = pltpu.make_async_copy(own_w, w_all.at[row], here.at[1])
    keep_w.start()
    w_out = [remote(own_w, w_all.at[row], ws.at[d], wr.at[d], to) for d, to in enumerate([sibling] + across)]
    for copy in w_out:
        copy.start()
    passed = []
    for out, whole, send, recv in ((tgt_out, tgt_all, fs, fr), (w_out, w_all, gs, gr)):
        for d in range(1, pairs):
            out[d].wait_recv()
            origin = lax.rem(pair - d + pairs, pairs) * 2 + half
            copy = remote(whole.at[origin], whole.at[origin], send.at[d], recv.at[d], sibling)
            copy.start()
            passed.append(copy)
        out[0].wait_recv()
        for copy in out:
            copy.wait_send()
    for copy in passed:
        copy.wait()
    keep.wait()
    keep_w.wait()


def gather_targets(nrow, looked, backward, tgt):
    seqs, cols = looked.shape
    part = seqs // nrow
    pairs = nrow // 2
    vmem = pl.BlockSpec(memory_space=pltpu.VMEM)
    hbm = pl.BlockSpec(memory_space=pl.ANY)
    dma = pltpu.SemaphoreType.DMA
    tgt_all, w_all = pl.pallas_call(
        functools.partial(gather_body, nrow),
        in_specs=[vmem, vmem, hbm],
        out_specs=[hbm, hbm],
        out_shape=[
            jax.ShapeDtypeStruct((nrow,) + tgt.shape, BF16),
            jax.ShapeDtypeStruct((nrow, part, cols), BF16),
        ],
        scratch_shapes=[
            pltpu.VMEM((pairs, part, cols), BF16),
            pltpu.VMEM((pairs, part, cols), BF16),
            pltpu.VMEM((part, cols), BF16),
        ]
        + [dma((pairs,))] * 12
        + [dma((2,))],
        compiler_params=pltpu.CompilerParams(
            collective_id=0, has_side_effects=True, vmem_limit_bytes=40 * MIB
        ),
        cost_estimate=pl.CostEstimate(flops=0, bytes_accessed=200 * MIB, transcendentals=0),
        name="gather_targets",
    )(looked.reshape(nrow, part, cols), backward, tgt)
    return tgt_all.reshape(nrow * tgt.shape[0], tgt.shape[1]), w_all.reshape(seqs, cols)


def first_pass(src, tgt, weighted):
    rows, width = src.shape
    cols = tgt.shape[0]
    seqs = weighted.shape[0]
    tile = fit(rows, 256)
    chunk = fit(cols, 2048)
    tiles = rows // tile

    def body(src_ref, tgt_ref, w_ref, e_ref, reach_ref, peak_ref, sum_ref, s0, s1, p0, p1):
        step = pl.program_id(0)

        def run(new, old, new_peak, old_peak):
            peak = old_peak[...]
            reach_ref[...] = jnp.zeros_like(reach_ref)

            def go(c, carry):
                best, total = carry
                at = pl.ds(pl.multiple_of(c * chunk, chunk), chunk)
                logits = lax.dot_general(src_ref[...], tgt_ref[at, :], NT, preferred_element_type=F32)
                new[:, at] = logits
                best = jnp.maximum(best, jnp.max(logits, axis=1, keepdims=True))
                e = jnp.exp(old[:, at] - peak)
                total = total + jnp.sum(e, axis=1, keepdims=True)
                eb = e.astype(BF16)
                e_ref[:, at] = eb
                reach_ref[...] += lax.dot_general(w_ref[:, at], eb, NT, preferred_element_type=F32)
                return best, total

            best, total = lax.fori_loop(
                0, cols // chunk, go, (jnp.full((tile, 1), -jnp.inf, F32), jnp.zeros((tile, 1), F32))
            )
            new_peak[...] = best
            sum_ref[...] = to_row(total)
            peak_ref[...] = to_row(peak)

        @pl.when(lax.rem(step, 2) == 0)
        def _():
            run(s0, s1, p0, p1)

        @pl.when(lax.rem(step, 2) == 1)
        def _():
            run(s1, s0, p1, p0)

    once = pl.Buffered(1)
    behind = lambda t: (jnp.maximum(t - 1, 0), 0)
    beside = lambda t: (0, jnp.maximum(t - 1, 0))
    whole = lambda t: (0, 0)
    return pl.pallas_call(
        body,
        grid=(tiles + 1,),
        in_specs=[
            pl.BlockSpec((tile, width), lambda t: (jnp.minimum(t, tiles - 1), 0)),
            pl.BlockSpec((cols, width), whole, pipeline_mode=once),
            pl.BlockSpec((seqs, cols), whole, pipeline_mode=once),
        ],
        out_specs=[
            pl.BlockSpec((tile, cols), behind),
            pl.BlockSpec((seqs, tile), beside),
            pl.BlockSpec((1, tile), beside),
            pl.BlockSpec((1, tile), beside),
        ],
        out_shape=[
            jax.ShapeDtypeStruct((rows, cols), BF16),
            jax.ShapeDtypeStruct((seqs, rows), F32),
            jax.ShapeDtypeStruct((1, rows), F32),
            jax.ShapeDtypeStruct((1, rows), F32),
        ],
        scratch_shapes=[
            pltpu.VMEM((tile, cols), F32),
            pltpu.VMEM((tile, cols), F32),
            pltpu.VMEM((tile, 1), F32),
            pltpu.VMEM((tile, 1), F32),
        ],
        compiler_params=pltpu.CompilerParams(
            dimension_semantics=("arbitrary",), vmem_limit_bytes=58 * MIB
        ),
        cost_estimate=pl.CostEstimate(
            flops=2 * rows * cols * (width + seqs), bytes_accessed=200 * MIB, transcendentals=rows * cols
        ),
        name="first_pass",
    )(src, tgt, weighted)


def weights_body(nrow, ncol, factor, chunk, peak, sums, reach, fwd, coeffs, share,
                 stats, terms_col, terms_row, counts, rate, *sems):
    (a_s, a_r, b_s, b_r, c_s, c_r, d_s, d_r) = sems
    row, col = lax.axis_index("row"), lax.axis_index("col")
    cols = [(row, lax.rem(col + d, ncol)) for d in range(1, ncol)]
    rows = [(lax.rem(row + d, nrow), col) for d in range(1, nrow)]
    greet(cols + rows)
    size = reach.shape[1]

    def share_out(buffer, send, recv, devices):
        copies = [
            remote(buffer.at[0], buffer.at[d + 1], send.at[d], recv.at[d], to) for d, to in enumerate(devices)
        ]
        for copy in copies:
            copy.start()
        for copy in copies:
            copy.wait()

    stats[0, 0:1, :] = peak[...]
    stats[0, 1:2, :] = sums[...]
    share_out(stats, a_s, a_r, cols)
    best = stats[0, 0:1, :]
    for d in range(1, ncol):
        best = jnp.maximum(best, stats[d, 0:1, :])
    total = jnp.zeros_like(best)
    for d in range(ncol):
        total = total + stats[d, 1:2, :] * jnp.exp(stats[d, 0:1, :] - best)
    rate[0:1, :] = jnp.exp(peak[...] - best) / total

    def norm(c, carry):
        at = pl.ds(pl.multiple_of(c * chunk, chunk), chunk)
        term = fwd[:, at].astype(F32) * reach[:, at] * rate[0:1, at]
        return carry + jnp.sum(term, axis=1, keepdims=True)

    seqs = reach.shape[0]
    terms = lax.fori_loop(0, size // chunk, norm, jnp.zeros((seqs, 1), F32))
    terms_col[0] = to_row(terms)
    share_out(terms_col, b_s, b_r, cols)
    part = terms_col[0]
    for d in range(1, ncol):
        part = part + terms_col[d]
    terms_row[0] = part
    share_out(terms_row, c_s, c_r, rows)
    part = terms_row[0]
    for d in range(1, nrow):
        part = part + terms_row[d]
    inverse = to_column(factor / part)

    def weigh(c, carry):
        at = pl.ds(pl.multiple_of(c * chunk, chunk), chunk)
        made = (fwd[:, at].astype(F32) * inverse * rate[0:1, at]).astype(BF16)
        coeffs[:, at] = made
        counts[0, :, at] = jnp.sum(made.astype(F32) * reach[:, at], axis=0, keepdims=True)
        return carry

    lax.fori_loop(0, size // chunk, weigh, 0)
    share_out(counts, d_s, d_r, cols)
    count = counts[0]
    for d in range(1, ncol):
        count = count + counts[d]
    share[...] = count * rate[0:1, :]


def make_weights(nrow, ncol, factor, peak, sums, reach, forward):
    seqs, rows = reach.shape
    vmem = pl.BlockSpec(memory_space=pltpu.VMEM)
    dma = pltpu.SemaphoreType.DMA
    return pl.pallas_call(
        functools.partial(weights_body, nrow, ncol, factor, fit(rows, 512)),
        in_specs=[vmem] * 4,
        out_specs=[vmem] * 2,
        out_shape=[jax.ShapeDtypeStruct((seqs, rows), BF16), jax.ShapeDtypeStruct((1, rows), F32)],
        scratch_shapes=[
            pltpu.VMEM((ncol, 2, rows), F32),
            pltpu.VMEM((ncol, 1, seqs), F32),
            pltpu.VMEM((nrow, 1, seqs), F32),
            pltpu.VMEM((ncol, 1, rows), F32),
            pltpu.VMEM((1, rows), F32),
        ]
        + [dma((ncol - 1,))] * 4
        + [dma((nrow - 1,))] * 2
        + [dma((ncol - 1,))] * 2,
        compiler_params=pltpu.CompilerParams(
            collective_id=1, has_side_effects=True, vmem_limit_bytes=40 * MIB
        ),
        cost_estimate=pl.CostEstimate(flops=0, bytes_accessed=30 * MIB, transcendentals=0),
        name="make_weights",
    )(peak, sums, reach, forward)


def second_pass(exp_block, coeffs, share, weighted, tgt, src):
    rows, cols = exp_block.shape
    width = tgt.shape[1]
    seqs = weighted.shape[0]
    tile = fit(rows, 512)
    chunk = fit(cols, 512)
    group = 4 if (cols // chunk) % 4 == 0 else 1
    tiles = rows // tile
    turn = fit(cols, 1024)

    def body(e_ref, c_ref, share_ref, w_ref, tgt_ref, src_ref, gs_ref, gt_ref, total_ref):
        step = pl.program_id(0)

        @pl.when(step == 0)
        def _():
            total_ref[...] = jnp.zeros_like(total_ref)

        lead = c_ref[...].astype(F32).T.astype(BF16)
        flipped = src_ref[...].astype(F32).T.astype(BF16)
        level = to_column(share_ref[...])

        def go(c, total):
            for k in range(group):
                at = pl.ds(pl.multiple_of((c * group + k) * chunk, chunk), chunk)
                summed = jnp.dot(lead, w_ref[:, at], preferred_element_type=F32)
                g = (e_ref[:, at].astype(F32) * (summed - level)).astype(BF16)
                total = total + jnp.dot(g, tgt_ref[at, :], preferred_element_type=F32)
                total_ref[:, at] += jnp.dot(flipped, g, preferred_element_type=F32)
            return total

        made = lax.fori_loop(0, cols // chunk // group, go, jnp.zeros((tile, width), F32))
        gs_ref[...] = made.astype(BF16)

        @pl.when(step == tiles - 1)
        def _():
            def flip(c, carry):
                at = pl.ds(pl.multiple_of(c * turn, turn), turn)
                gt_ref[at, :] = total_ref[:, at].T.astype(BF16)
                return carry

            lax.fori_loop(0, cols // turn, flip, 0)

    once = pl.Buffered(1)
    by_row = lambda t: (t, 0)
    beside = lambda t: (0, t)
    whole = lambda t: (0, 0)
    return pl.pallas_call(
        body,
        grid=(tiles,),
        in_specs=[
            pl.BlockSpec((tile, cols), by_row),
            pl.BlockSpec((seqs, tile), beside),
            pl.BlockSpec((1, tile), beside),
            pl.BlockSpec((seqs, cols), whole, pipeline_mode=once),
            pl.BlockSpec((cols, width), whole, pipeline_mode=once),
            pl.BlockSpec((tile, width), by_row),
        ],
        out_specs=[
            pl.BlockSpec((tile, width), by_row),
            pl.BlockSpec((cols, width), whole, pipeline_mode=once),
        ],
        out_shape=[
            jax.ShapeDtypeStruct((rows, width), BF16),
            jax.ShapeDtypeStruct((cols, width), BF16),
        ],
        scratch_shapes=[pltpu.VMEM((width, cols), F32)],
        compiler_params=pltpu.CompilerParams(
            dimension_semantics=("arbitrary",), vmem_limit_bytes=58 * MIB
        ),
        cost_estimate=pl.CostEstimate(
            flops=2 * rows * cols * (2 * width + seqs), bytes_accessed=100 * MIB, transcendentals=0
        ),
        name="second_pass",
    )(exp_block, coeffs, share, weighted, tgt, src)


def scatter_body(nrow, ncol, ps, pt, out_src, out_tgt, col_in, pair_in, pair_out, chip_in, *sems):
    (a_s, a_r, b_s, b_r, c_s, c_r) = sems
    pairs = nrow // 2
    row, half, pair, sibling, across = row_peers(nrow)
    col = lax.axis_index("col")
    places = [lax.rem(col + d, ncol) for d in range(1, ncol)]
    greet([sibling] + across + [(row, place) for place in places])
    first = [remote(pt.at[2 * q + 1 - half], pair_in.at[q], b_s.at[q], b_r.at[q], sibling) for q in range(pairs)]
    for copy in first:
        copy.start()
    along = [
        remote(ps.at[place], col_in.at[d], a_s.at[d], a_r.at[d], (row, place)) for d, place in enumerate(places)
    ]
    for copy in along:
        copy.start()
    for copy in first:
        copy.wait()
    for d in range(1, pairs):
        q = lax.rem(pair + d, pairs)
        pair_out[d] = (pt[2 * q + half].astype(F32) + pair_in[q].astype(F32)).astype(BF16)
    second = [remote(pair_out.at[d], chip_in.at[d], c_s.at[d], c_r.at[d], across[d - 1]) for d in range(1, pairs)]
    for copy in second:
        copy.start()
    total = pt[2 * pair + half].astype(F32) + pair_in[pair].astype(F32)
    for d, copy in enumerate(second):
        copy.wait()
        total = total + chip_in[d + 1].astype(F32)
    out_tgt[...] = total
    total = ps[col].astype(F32)
    for d, copy in enumerate(along):
        copy.wait()
        total = total + col_in[d].astype(F32)
    out_src[...] = total


def scatter_sums(nrow, ncol, part_src, part_tgt):
    width = part_src.shape[1]
    src_rows = part_src.shape[0] // ncol
    tgt_rows = part_tgt.shape[0] // nrow
    pairs = nrow // 2
    vmem = pl.BlockSpec(memory_space=pltpu.VMEM)
    dma = pltpu.SemaphoreType.DMA
    return pl.pallas_call(
        functools.partial(scatter_body, nrow, ncol),
        in_specs=[vmem] * 2,
        out_specs=[vmem] * 2,
        out_shape=[
            jax.ShapeDtypeStruct((src_rows, width), F32),
            jax.ShapeDtypeStruct((tgt_rows, width), F32),
        ],
        scratch_shapes=[
            pltpu.VMEM((ncol - 1, src_rows, width), BF16),
            pltpu.VMEM((pairs, tgt_rows, width), BF16),
            pltpu.VMEM((pairs, tgt_rows, width), BF16),
            pltpu.VMEM((pairs, tgt_rows, width), BF16),
        ]
        + [dma((ncol - 1,))] * 2
        + [dma((pairs,))] * 4,
        compiler_params=pltpu.CompilerParams(
            collective_id=2, has_side_effects=True, vmem_limit_bytes=40 * MIB
        ),
        cost_estimate=pl.CostEstimate(flops=0, bytes_accessed=100 * MIB, transcendentals=0),
        name="scatter_sums",
    )(part_src.reshape(ncol, src_rows, width), part_tgt.reshape(nrow, tgt_rows, width))


def on_device(nrow, ncol, tokens, emission_table, forward_rows, backward_rows, src_embed, tgt_embed):
    src_block = lax.all_gather(src_embed, "col", axis=0, tiled=True)
    forward_all = lax.all_gather(forward_rows, "col", axis=0, tiled=True)
    vocab_local = emission_table.shape[0]
    offset = lax.axis_index("row") * vocab_local
    onehot = (tokens[:, None] == offset + jnp.arange(vocab_local, dtype=jnp.int32)[None, :]).astype(BF16)
    looked = jnp.dot(onehot, emission_table, preferred_element_type=F32).astype(BF16)
    tgt_block, weighted = gather_targets(nrow, looked, backward_rows, tgt_embed)
    exp_block, reach, peak, sums = first_pass(src_block, tgt_block, weighted)
    factor = forward_rows.shape[1] * nrow / tokens.shape[0]
    coeffs, share = make_weights(nrow, ncol, factor, peak, sums, reach, forward_all)
    part_src, part_tgt = second_pass(exp_block, coeffs, share, weighted, tgt_block, src_block)
    return scatter_sums(nrow, ncol, part_src, part_tgt)


def solution(mesh):
    in_specs = (
        P(),
        P("row", "col"),
        P("col", "row"),
        P("row", "col"),
        P(("row", "col"), None),
        P(("col", "row"), None),
    )
    out_specs = (P(("row", "col"), None), P(("col", "row"), None))
    return jax.shard_map(
        functools.partial(on_device, mesh.shape["row"], mesh.shape["col"]),
        mesh=mesh,
        in_specs=in_specs,
        out_specs=out_specs,
        check_vma=False,
    )
```

```python
import functools

import jax
import jax.numpy as jnp
from jax import lax
from jax.experimental import pallas as pl
from jax.experimental.pallas import tpu as pltpu
from jax.sharding import PartitionSpec as P

NT = (((1,), (1,)), ((), ()))
BF16 = jnp.bfloat16
F32 = jnp.float32
MESH = pl.DeviceIdType.MESH
MIB = 1024 * 1024


def fit(size, want):
    while size % want:
        want //= 2
    return want


def to_row(column):
    return jnp.broadcast_to(column, (column.shape[0], 128)).T[:1]


def to_column(row):
    return jnp.broadcast_to(row, (128, row.shape[1])).T[:, :1]


def remote(src, dst, send, recv, device):
    return pltpu.make_async_remote_copy(
        src_ref=src, dst_ref=dst, send_sem=send, recv_sem=recv, device_id=device, device_id_type=MESH
    )


def greet(devices):
    barrier = pltpu.get_barrier_semaphore()
    for device in devices:
        pl.semaphore_signal(barrier, inc=1, device_id=device, device_id_type=MESH)
    pl.semaphore_wait(barrier, len(devices))


def row_peers(nrow):
    row, col = lax.axis_index("row"), lax.axis_index("col")
    half, pair, pairs = lax.rem(row, 2), row // 2, nrow // 2
    sibling = (pair * 2 + 1 - half, col)
    across = [(lax.rem(pair + d, pairs) * 2 + half, col) for d in range(1, pairs)]
    return row, half, pair, sibling, across


def gather_body(nrow, looked, tgt, tgt_all, pair_sum, pair_in, *sems):
    (s1, r1, ts, tr, fs, fr, here) = sems
    pairs = nrow // 2
    row, half, pair, sibling, across = row_peers(nrow)
    greet([sibling] + across)

    tgt_out = [remote(tgt, tgt_all.at[row], ts.at[d], tr.at[d], to) for d, to in enumerate([sibling] + across)]
    for copy in tgt_out:
        copy.start()
    keep = pltpu.make_async_copy(tgt, tgt_all.at[row], here)
    keep.start()
    first = [remote(looked.at[2 * q + 1 - half], pair_in.at[q], s1.at[q], r1.at[q], sibling) for q in range(pairs)]
    for copy in first:
        copy.start()
    for q, copy in enumerate(first):
        copy.wait()
        pair_sum[q] = (looked[2 * q + half].astype(F32) + pair_in[q].astype(F32)).astype(BF16)
    passed = []
    for d in range(1, pairs):
        tgt_out[d].wait_recv()
        origin = lax.rem(pair - d + pairs, pairs) * 2 + half
        copy = remote(tgt_all.at[origin], tgt_all.at[origin], fs.at[d], fr.at[d], sibling)
        copy.start()
        passed.append(copy)
    tgt_out[0].wait_recv()
    for copy in tgt_out:
        copy.wait_send()
    for copy in passed:
        copy.wait()
    keep.wait()


def gather_targets(nrow, looked, tgt):
    seqs, cols = looked.shape
    part = seqs // nrow
    pairs = nrow // 2
    vmem = pl.BlockSpec(memory_space=pltpu.VMEM)
    hbm = pl.BlockSpec(memory_space=pl.ANY)
    dma = pltpu.SemaphoreType.DMA
    tgt_all, pair_sum = pl.pallas_call(
        functools.partial(gather_body, nrow),
        in_specs=[vmem, hbm],
        out_specs=[hbm, vmem],
        out_shape=[
            jax.ShapeDtypeStruct((nrow,) + tgt.shape, BF16),
            jax.ShapeDtypeStruct((pairs, part, cols), BF16),
        ],
        scratch_shapes=[pltpu.VMEM((pairs, part, cols), BF16)] + [dma((pairs,))] * 6 + [dma],
        compiler_params=pltpu.CompilerParams(
            collective_id=0, has_side_effects=True, vmem_limit_bytes=40 * MIB
        ),
        cost_estimate=pl.CostEstimate(flops=0, bytes_accessed=100 * MIB, transcendentals=0),
        name="gather_targets",
    )(looked.reshape(nrow, part, cols), tgt)
    return tgt_all.reshape(nrow * tgt.shape[0], tgt.shape[1]), pair_sum


def exp_body(nrow, tiles, chunk, src_ref, tgt_ref, pair_sum, back, e_ref, peak_ref, sum_ref, w_all,
             s0, s1, p0, p1, chip_in, own_w, *sems):
    (s2, r2, ws, wr, gs, gr, here) = sems
    pairs = nrow // 2
    row, half, pair, sibling, across = row_peers(nrow)
    step = pl.program_id(0)
    tile, cols = e_ref.shape

    second = [
        remote(pair_sum.at[lax.rem(pair + d, pairs)], chip_in.at[d], s2.at[d], r2.at[d], across[d - 1])
        for d in range(1, pairs)
    ]
    keep = pltpu.make_async_copy(own_w, w_all.at[row], here)
    out = [remote(own_w, w_all.at[row], ws.at[d], wr.at[d], to) for d, to in enumerate([sibling] + across)]
    passed = []
    for d in range(1, pairs):
        origin = lax.rem(pair - d + pairs, pairs) * 2 + half
        passed.append(remote(w_all.at[origin], w_all.at[origin], gs.at[d], gr.at[d], sibling))

    @pl.when(step == 0)
    def _():
        greet([sibling] + across)
        for copy in second:
            copy.start()

    @pl.when(step == max(tiles // 2 - 1, 0))
    def _():
        looks = pair_sum[pair].astype(F32)
        for d, copy in enumerate(second):
            copy.wait()
            looks = looks + chip_in[d + 1].astype(F32)
        own_w[...] = (jnp.exp(looks) * back[...].astype(F32)).astype(BF16)
        for copy in out:
            copy.start()
        keep.start()

    @pl.when(step == tiles - 1)
    def _():
        for copy, along in zip(out[1:], passed):
            copy.wait_recv()
            along.start()

    def run(new, old, new_peak, old_peak):
        peak = old_peak[...]

        def go(c, carry):
            best, total = carry
            at = pl.ds(pl.multiple_of(c * chunk, chunk), chunk)
            logits = lax.dot_general(src_ref[...], tgt_ref[at, :], NT, preferred_element_type=F32)
            new[:, at] = logits
            best = jnp.maximum(best, jnp.max(logits, axis=1, keepdims=True))
            e = jnp.exp(old[:, at] - peak)
            e_ref[:, at] = e.astype(BF16)
            return best, total + jnp.sum(e, axis=1, keepdims=True)

        best, total = lax.fori_loop(
            0, cols // chunk, go, (jnp.full((tile, 1), -jnp.inf, F32), jnp.zeros((tile, 1), F32))
        )
        new_peak[...] = best
        sum_ref[...] = to_row(total)
        peak_ref[...] = to_row(peak)

    @pl.when(lax.rem(step, 2) == 0)
    def _():
        run(s0, s1, p0, p1)

    @pl.when(lax.rem(step, 2) == 1)
    def _():
        run(s1, s0, p1, p0)

    @pl.when(step == tiles)
    def _():
        out[0].wait_recv()
        for copy in out:
            copy.wait_send()
        for copy in passed:
            copy.wait()
        keep.wait()


def exp_pass(nrow, src, tgt, pair_sum, backward):
    rows, width = src.shape
    cols = tgt.shape[0]
    pairs, part = pair_sum.shape[:2]
    tile = fit(rows, 256)
    chunk = fit(cols, 2048)
    tiles = rows // tile
    once = pl.Buffered(1)
    behind = lambda t: (jnp.maximum(t - 1, 0), 0)
    beside = lambda t: (0, jnp.maximum(t - 1, 0))
    whole = lambda t: (0, 0)
    dma = pltpu.SemaphoreType.DMA
    exp_block, peak, sums, w_all = pl.pallas_call(
        functools.partial(exp_body, nrow, tiles, chunk),
        grid=(tiles + 1,),
        in_specs=[
            pl.BlockSpec((tile, width), lambda t: (jnp.minimum(t, tiles - 1), 0)),
            pl.BlockSpec((cols, width), whole, pipeline_mode=once),
            pl.BlockSpec(pair_sum.shape, lambda t: (0, 0, 0), pipeline_mode=once),
            pl.BlockSpec(backward.shape, whole, pipeline_mode=once),
        ],
        out_specs=[
            pl.BlockSpec((tile, cols), behind),
            pl.BlockSpec((1, tile), beside),
            pl.BlockSpec((1, tile), beside),
            pl.BlockSpec(memory_space=pl.ANY),
        ],
        out_shape=[
            jax.ShapeDtypeStruct((rows, cols), BF16),
            jax.ShapeDtypeStruct((1, rows), F32),
            jax.ShapeDtypeStruct((1, rows), F32),
            jax.ShapeDtypeStruct((nrow, part, cols), BF16),
        ],
        scratch_shapes=[
            pltpu.VMEM((tile, cols), F32),
            pltpu.VMEM((tile, cols), F32),
            pltpu.VMEM((tile, 1), F32),
            pltpu.VMEM((tile, 1), F32),
            pltpu.VMEM((pairs, part, cols), BF16),
            pltpu.VMEM((part, cols), BF16),
        ]
        + [dma((pairs,))] * 6
        + [dma],
        compiler_params=pltpu.CompilerParams(
            dimension_semantics=("arbitrary",), collective_id=3, has_side_effects=True, vmem_limit_bytes=58 * MIB
        ),
        cost_estimate=pl.CostEstimate(
            flops=2 * rows * cols * width, bytes_accessed=200 * MIB, transcendentals=rows * cols
        ),
        name="exp_pass",
    )(src, tgt, pair_sum, backward)
    return exp_block, peak, sums, w_all.reshape(nrow * part, cols)


def reach_pass(exp_block, weighted):
    rows, cols = exp_block.shape
    seqs = weighted.shape[0]
    tile = fit(rows, 512)
    chunk = fit(cols, 2048)

    def body(w_ref, e_ref, reach_ref):
        total = jnp.zeros(reach_ref.shape, F32)
        for c in range(cols // chunk):
            at = pl.ds(c * chunk, chunk)
            total = total + lax.dot_general(w_ref[:, at], e_ref[:, at], NT, preferred_element_type=F32)
        reach_ref[...] = total

    return pl.pallas_call(
        body,
        grid=(rows // tile,),
        in_specs=[
            pl.BlockSpec((seqs, cols), lambda t: (0, 0), pipeline_mode=pl.Buffered(1)),
            pl.BlockSpec((tile, cols), lambda t: (t, 0)),
        ],
        out_specs=pl.BlockSpec((seqs, tile), lambda t: (0, t)),
        out_shape=jax.ShapeDtypeStruct((seqs, rows), F32),
        compiler_params=pltpu.CompilerParams(
            dimension_semantics=("arbitrary",), vmem_limit_bytes=58 * MIB
        ),
        cost_estimate=pl.CostEstimate(flops=2 * rows * cols * seqs, bytes_accessed=2 * rows * cols, transcendentals=0),
        name="reach_pass",
    )(weighted, exp_block)


def weights_body(nrow, ncol, factor, chunk, peak, sums, reach, fwd, coeffs, share,
                 stats, terms_col, terms_row, counts, rate, *sems):
    (a_s, a_r, b_s, b_r, c_s, c_r, d_s, d_r) = sems
    row, col = lax.axis_index("row"), lax.axis_index("col")
    cols = [(row, lax.rem(col + d, ncol)) for d in range(1, ncol)]
    rows = [(lax.rem(row + d, nrow), col) for d in range(1, nrow)]
    greet(cols + rows)
    size = reach.shape[1]

    def share_out(buffer, send, recv, devices):
        copies = [
            remote(buffer.at[0], buffer.at[d + 1], send.at[d], recv.at[d], to) for d, to in enumerate(devices)
        ]
        for copy in copies:
            copy.start()
        for copy in copies:
            copy.wait()

    stats[0, 0:1, :] = peak[...]
    stats[0, 1:2, :] = sums[...]
    share_out(stats, a_s, a_r, cols)
    best = stats[0, 0:1, :]
    for d in range(1, ncol):
        best = jnp.maximum(best, stats[d, 0:1, :])
    total = jnp.zeros_like(best)
    for d in range(ncol):
        total = total + stats[d, 1:2, :] * jnp.exp(stats[d, 0:1, :] - best)
    rate[0:1, :] = jnp.exp(peak[...] - best) / total

    def norm(c, carry):
        at = pl.ds(pl.multiple_of(c * chunk, chunk), chunk)
        term = fwd[:, at].astype(F32) * reach[:, at] * rate[0:1, at]
        return carry + jnp.sum(term, axis=1, keepdims=True)

    seqs = reach.shape[0]
    terms = lax.fori_loop(0, size // chunk, norm, jnp.zeros((seqs, 1), F32))
    terms_col[0] = to_row(terms)
    share_out(terms_col, b_s, b_r, cols)
    part = terms_col[0]
    for d in range(1, ncol):
        part = part + terms_col[d]
    terms_row[0] = part
    share_out(terms_row, c_s, c_r, rows)
    part = terms_row[0]
    for d in range(1, nrow):
        part = part + terms_row[d]
    inverse = to_column(factor / part)

    def weigh(c, carry):
        at = pl.ds(pl.multiple_of(c * chunk, chunk), chunk)
        made = (fwd[:, at].astype(F32) * inverse * rate[0:1, at]).astype(BF16)
        coeffs[:, at] = made
        counts[0, :, at] = jnp.sum(made.astype(F32) * reach[:, at], axis=0, keepdims=True)
        return carry

    lax.fori_loop(0, size // chunk, weigh, 0)
    share_out(counts, d_s, d_r, cols)
    count = counts[0]
    for d in range(1, ncol):
        count = count + counts[d]
    share[...] = count * rate[0:1, :]


def make_weights(nrow, ncol, factor, peak, sums, reach, forward):
    seqs, rows = reach.shape
    vmem = pl.BlockSpec(memory_space=pltpu.VMEM)
    dma = pltpu.SemaphoreType.DMA
    return pl.pallas_call(
        functools.partial(weights_body, nrow, ncol, factor, fit(rows, 512)),
        in_specs=[vmem] * 4,
        out_specs=[vmem] * 2,
        out_shape=[jax.ShapeDtypeStruct((seqs, rows), BF16), jax.ShapeDtypeStruct((1, rows), F32)],
        scratch_shapes=[
            pltpu.VMEM((ncol, 2, rows), F32),
            pltpu.VMEM((ncol, 1, seqs), F32),
            pltpu.VMEM((nrow, 1, seqs), F32),
            pltpu.VMEM((ncol, 1, rows), F32),
            pltpu.VMEM((1, rows), F32),
        ]
        + [dma((ncol - 1,))] * 4
        + [dma((nrow - 1,))] * 2
        + [dma((ncol - 1,))] * 2,
        compiler_params=pltpu.CompilerParams(
            collective_id=1, has_side_effects=True, vmem_limit_bytes=40 * MIB
        ),
        cost_estimate=pl.CostEstimate(flops=0, bytes_accessed=30 * MIB, transcendentals=0),
        name="make_weights",
    )(peak, sums, reach, forward)


def second_pass(exp_block, coeffs, share, weighted, tgt, src):
    rows, cols = exp_block.shape
    width = tgt.shape[1]
    seqs = weighted.shape[0]
    tile = fit(rows, 512)
    chunk = fit(cols, 1024)
    tiles = rows // tile
    turn = fit(cols, 1024)

    def body(e_ref, c_ref, share_ref, w_ref, tgt_ref, src_ref, gs_ref, gt_ref, total_ref):
        step = pl.program_id(0)

        @pl.when(step == 0)
        def _():
            total_ref[...] = jnp.zeros_like(total_ref)

        lead = c_ref[...].astype(F32).T.astype(BF16)
        flipped = src_ref[...].astype(F32).T.astype(BF16)
        level = to_column(share_ref[...])

        def make(c):
            at = pl.ds(c * chunk, chunk)
            summed = jnp.dot(lead, w_ref[:, at], preferred_element_type=F32)
            return (e_ref[:, at].astype(F32) * (summed - level)).astype(BF16)

        made = jnp.zeros((tile, width), F32)
        ahead = make(0)
        for c in range(cols // chunk):
            g = ahead
            if c + 1 < cols // chunk:
                ahead = make(c + 1)
            at = pl.ds(c * chunk, chunk)
            made = made + jnp.dot(g, tgt_ref[at, :], preferred_element_type=F32)
            total_ref[:, at] += jnp.dot(flipped, g, preferred_element_type=F32)
        gs_ref[...] = made.astype(BF16)

        @pl.when(step == tiles - 1)
        def _():
            def flip(c, carry):
                at = pl.ds(pl.multiple_of(c * turn, turn), turn)
                gt_ref[at, :] = total_ref[:, at].T.astype(BF16)
                return carry

            lax.fori_loop(0, cols // turn, flip, 0)

    once = pl.Buffered(1)
    by_row = lambda t: (t, 0)
    beside = lambda t: (0, t)
    whole = lambda t: (0, 0)
    return pl.pallas_call(
        body,
        grid=(tiles,),
        in_specs=[
            pl.BlockSpec((tile, cols), by_row),
            pl.BlockSpec((seqs, tile), beside),
            pl.BlockSpec((1, tile), beside),
            pl.BlockSpec((seqs, cols), whole, pipeline_mode=once),
            pl.BlockSpec((cols, width), whole, pipeline_mode=once),
            pl.BlockSpec((tile, width), by_row),
        ],
        out_specs=[
            pl.BlockSpec((tile, width), by_row),
            pl.BlockSpec((cols, width), whole, pipeline_mode=once),
        ],
        out_shape=[
            jax.ShapeDtypeStruct((rows, width), BF16),
            jax.ShapeDtypeStruct((cols, width), BF16),
        ],
        scratch_shapes=[pltpu.VMEM((width, cols), F32)],
        compiler_params=pltpu.CompilerParams(
            dimension_semantics=("arbitrary",), vmem_limit_bytes=58 * MIB
        ),
        cost_estimate=pl.CostEstimate(
            flops=2 * rows * cols * (2 * width + seqs), bytes_accessed=100 * MIB, transcendentals=0
        ),
        name="second_pass",
    )(exp_block, coeffs, share, weighted, tgt, src)


def scatter_body(nrow, ncol, ps, pt, out_src, out_tgt, col_in, pair_in, pair_out, chip_in, *sems):
    (a_s, a_r, b_s, b_r, c_s, c_r) = sems
    pairs = nrow // 2
    row, half, pair, sibling, across = row_peers(nrow)
    col = lax.axis_index("col")
    places = [lax.rem(col + d, ncol) for d in range(1, ncol)]
    greet([sibling] + across + [(row, place) for place in places])
    first = [remote(pt.at[2 * q + 1 - half], pair_in.at[q], b_s.at[q], b_r.at[q], sibling) for q in range(pairs)]
    for copy in first:
        copy.start()
    along = [
        remote(ps.at[place], col_in.at[d], a_s.at[d], a_r.at[d], (row, place)) for d, place in enumerate(places)
    ]
    for copy in along:
        copy.start()
    for copy in first:
        copy.wait()
    for d in range(1, pairs):
        q = lax.rem(pair + d, pairs)
        pair_out[d] = (pt[2 * q + half].astype(F32) + pair_in[q].astype(F32)).astype(BF16)
    second = [remote(pair_out.at[d], chip_in.at[d], c_s.at[d], c_r.at[d], across[d - 1]) for d in range(1, pairs)]
    for copy in second:
        copy.start()
    total = pt[2 * pair + half].astype(F32) + pair_in[pair].astype(F32)
    for d, copy in enumerate(second):
        copy.wait()
        total = total + chip_in[d + 1].astype(F32)
    out_tgt[...] = total
    total = ps[col].astype(F32)
    for d, copy in enumerate(along):
        copy.wait()
        total = total + col_in[d].astype(F32)
    out_src[...] = total


def scatter_sums(nrow, ncol, part_src, part_tgt):
    width = part_src.shape[1]
    src_rows = part_src.shape[0] // ncol
    tgt_rows = part_tgt.shape[0] // nrow
    pairs = nrow // 2
    vmem = pl.BlockSpec(memory_space=pltpu.VMEM)
    dma = pltpu.SemaphoreType.DMA
    return pl.pallas_call(
        functools.partial(scatter_body, nrow, ncol),
        in_specs=[vmem] * 2,
        out_specs=[vmem] * 2,
        out_shape=[
            jax.ShapeDtypeStruct((src_rows, width), F32),
            jax.ShapeDtypeStruct((tgt_rows, width), F32),
        ],
        scratch_shapes=[
            pltpu.VMEM((ncol - 1, src_rows, width), BF16),
            pltpu.VMEM((pairs, tgt_rows, width), BF16),
            pltpu.VMEM((pairs, tgt_rows, width), BF16),
            pltpu.VMEM((pairs, tgt_rows, width), BF16),
        ]
        + [dma((ncol - 1,))] * 2
        + [dma((pairs,))] * 4,
        compiler_params=pltpu.CompilerParams(
            collective_id=2, has_side_effects=True, vmem_limit_bytes=40 * MIB
        ),
        cost_estimate=pl.CostEstimate(flops=0, bytes_accessed=100 * MIB, transcendentals=0),
        name="scatter_sums",
    )(part_src.reshape(ncol, src_rows, width), part_tgt.reshape(nrow, tgt_rows, width))


def on_device(nrow, ncol, tokens, emission_table, forward_rows, backward_rows, src_embed, tgt_embed):
    src_block = lax.all_gather(src_embed, "col", axis=0, tiled=True)
    forward_all = lax.all_gather(forward_rows, "col", axis=0, tiled=True)
    vocab_local = emission_table.shape[0]
    offset = lax.axis_index("row") * vocab_local
    onehot = (tokens[:, None] == offset + jnp.arange(vocab_local, dtype=jnp.int32)[None, :]).astype(BF16)
    looked = jnp.dot(onehot, emission_table, preferred_element_type=F32).astype(BF16)
    tgt_block, pair_sum = gather_targets(nrow, looked, tgt_embed)
    exp_block, peak, sums, weighted = exp_pass(nrow, src_block, tgt_block, pair_sum, backward_rows)
    reach = reach_pass(exp_block, weighted)
    factor = forward_rows.shape[1] * nrow / tokens.shape[0]
    coeffs, share = make_weights(nrow, ncol, factor, peak, sums, reach, forward_all)
    part_src, part_tgt = second_pass(exp_block, coeffs, share, weighted, tgt_block, src_block)
    return scatter_sums(nrow, ncol, part_src, part_tgt)


def solution(mesh):
    in_specs = (
        P(),
        P("row", "col"),
        P("col", "row"),
        P("row", "col"),
        P(("row", "col"), None),
        P(("col", "row"), None),
    )
    out_specs = (P(("row", "col"), None), P(("col", "row"), None))
    return jax.shard_map(
        functools.partial(on_device, mesh.shape["row"], mesh.shape["col"]),
        mesh=mesh,
        in_specs=in_specs,
        out_specs=out_specs,
        check_vma=False,
    )
```

```python
import functools

import jax
import jax.numpy as jnp
from jax import lax
from jax.experimental import pallas as pl
from jax.experimental.pallas import tpu as pltpu
from jax.sharding import PartitionSpec as P

NT = (((1,), (1,)), ((), ()))
BF16 = jnp.bfloat16
F32 = jnp.float32
MESH = pl.DeviceIdType.MESH
MIB = 1024 * 1024


def fit(size, want):
    while size % want:
        want //= 2
    return want


def to_row(column):
    return jnp.broadcast_to(column, (column.shape[0], 128)).T[:1]


def to_column(row):
    return jnp.broadcast_to(row, (128, row.shape[1])).T[:, :1]


def remote(src, dst, send, recv, device):
    return pltpu.make_async_remote_copy(
        src_ref=src, dst_ref=dst, send_sem=send, recv_sem=recv, device_id=device, device_id_type=MESH
    )


def greet(devices):
    barrier = pltpu.get_barrier_semaphore()
    for device in devices:
        pl.semaphore_signal(barrier, inc=1, device_id=device, device_id_type=MESH)
    pl.semaphore_wait(barrier, len(devices))


def row_peers(nrow):
    row, col = lax.axis_index("row"), lax.axis_index("col")
    half, pair, pairs = lax.rem(row, 2), row // 2, nrow // 2
    sibling = (pair * 2 + 1 - half, col)
    across = [(lax.rem(pair + d, pairs) * 2 + half, col) for d in range(1, pairs)]
    return row, half, pair, sibling, across


def gather_body(nrow, looked, tgt, tgt_all, pair_sum, pair_in, *sems):
    (s1, r1, ts, tr, fs, fr, here) = sems
    pairs = nrow // 2
    row, half, pair, sibling, across = row_peers(nrow)
    greet([sibling] + across)

    tgt_out = [remote(tgt, tgt_all.at[row], ts.at[d], tr.at[d], to) for d, to in enumerate([sibling] + across)]
    for copy in tgt_out:
        copy.start()
    keep = pltpu.make_async_copy(tgt, tgt_all.at[row], here)
    keep.start()
    first = [remote(looked.at[2 * q + 1 - half], pair_in.at[q], s1.at[q], r1.at[q], sibling) for q in range(pairs)]
    for copy in first:
        copy.start()
    for q, copy in enumerate(first):
        copy.wait()
        pair_sum[q] = (looked[2 * q + half].astype(F32) + pair_in[q].astype(F32)).astype(BF16)
    passed = []
    for d in range(1, pairs):
        tgt_out[d].wait_recv()
        origin = lax.rem(pair - d + pairs, pairs) * 2 + half
        copy = remote(tgt_all.at[origin], tgt_all.at[origin], fs.at[d], fr.at[d], sibling)
        copy.start()
        passed.append(copy)
    tgt_out[0].wait_recv()
    for copy in tgt_out:
        copy.wait_send()
    for copy in passed:
        copy.wait()
    keep.wait()


def gather_targets(nrow, looked, tgt):
    seqs, cols = looked.shape
    part = seqs // nrow
    pairs = nrow // 2
    vmem = pl.BlockSpec(memory_space=pltpu.VMEM)
    hbm = pl.BlockSpec(memory_space=pl.ANY)
    dma = pltpu.SemaphoreType.DMA
    tgt_all, pair_sum = pl.pallas_call(
        functools.partial(gather_body, nrow),
        in_specs=[vmem, hbm],
        out_specs=[hbm, vmem],
        out_shape=[
            jax.ShapeDtypeStruct((nrow,) + tgt.shape, BF16),
            jax.ShapeDtypeStruct((pairs, part, cols), BF16),
        ],
        scratch_shapes=[pltpu.VMEM((pairs, part, cols), BF16)] + [dma((pairs,))] * 6 + [dma],
        compiler_params=pltpu.CompilerParams(
            collective_id=0, has_side_effects=True, vmem_limit_bytes=40 * MIB
        ),
        cost_estimate=pl.CostEstimate(flops=0, bytes_accessed=100 * MIB, transcendentals=0),
        name="gather_targets",
    )(looked.reshape(nrow, part, cols), tgt)
    return tgt_all.reshape(nrow * tgt.shape[0], tgt.shape[1]), pair_sum


def exp_body(nrow, tiles, chunk, src_ref, tgt_ref, pair_sum, back, e_ref, peak_ref, sum_ref, w_all,
             s0, s1, p0, p1, chip_in, own_w, *sems):
    (s2, r2, ws, wr, gs, gr, here) = sems
    pairs = nrow // 2
    row, half, pair, sibling, across = row_peers(nrow)
    step = pl.program_id(0)
    tile, cols = e_ref.shape

    second = [
        remote(pair_sum.at[lax.rem(pair + d, pairs)], chip_in.at[d], s2.at[d], r2.at[d], across[d - 1])
        for d in range(1, pairs)
    ]
    keep = pltpu.make_async_copy(own_w, w_all.at[row], here)
    out = [remote(own_w, w_all.at[row], ws.at[d], wr.at[d], to) for d, to in enumerate([sibling] + across)]
    passed = []
    for d in range(1, pairs):
        origin = lax.rem(pair - d + pairs, pairs) * 2 + half
        passed.append(remote(w_all.at[origin], w_all.at[origin], gs.at[d], gr.at[d], sibling))

    @pl.when(step == 0)
    def _():
        greet([sibling] + across)
        for copy in second:
            copy.start()

    @pl.when(step == max(tiles // 2 - 1, 0))
    def _():
        looks = pair_sum[pair].astype(F32)
        for d, copy in enumerate(second):
            copy.wait()
            looks = looks + chip_in[d + 1].astype(F32)
        own_w[...] = (jnp.exp(looks) * back[...].astype(F32)).astype(BF16)
        for copy in out:
            copy.start()
        keep.start()

    @pl.when(step == tiles - 1)
    def _():
        for copy, along in zip(out[1:], passed):
            copy.wait_recv()
            along.start()

    def run(new, old, new_peak, old_peak):
        peak = old_peak[...]

        def go(c, carry):
            best, total = carry
            at = pl.ds(pl.multiple_of(c * chunk, chunk), chunk)
            logits = lax.dot_general(src_ref[...], tgt_ref[at, :], NT, preferred_element_type=F32)
            new[:, at] = logits
            best = jnp.maximum(best, jnp.max(logits, axis=1, keepdims=True))
            e = jnp.exp(old[:, at] - peak)
            e_ref[:, at] = e.astype(BF16)
            return best, total + jnp.sum(e, axis=1, keepdims=True)

        best, total = lax.fori_loop(
            0, cols // chunk, go, (jnp.full((tile, 1), -jnp.inf, F32), jnp.zeros((tile, 1), F32)), unroll=2
        )
        new_peak[...] = best
        sum_ref[...] = to_row(total)
        peak_ref[...] = to_row(peak)

    @pl.when(lax.rem(step, 2) == 0)
    def _():
        run(s0, s1, p0, p1)

    @pl.when(lax.rem(step, 2) == 1)
    def _():
        run(s1, s0, p1, p0)

    @pl.when(step == tiles)
    def _():
        out[0].wait_recv()
        for copy in out:
            copy.wait_send()
        for copy in passed:
            copy.wait()
        keep.wait()


def exp_pass(nrow, src, tgt, pair_sum, backward):
    rows, width = src.shape
    cols = tgt.shape[0]
    pairs, part = pair_sum.shape[:2]
    tile = fit(rows, 256)
    chunk = fit(cols, 2048)
    tiles = rows // tile
    once = pl.Buffered(1)
    behind = lambda t: (jnp.maximum(t - 1, 0), 0)
    beside = lambda t: (0, jnp.maximum(t - 1, 0))
    whole = lambda t: (0, 0)
    dma = pltpu.SemaphoreType.DMA
    exp_block, peak, sums, w_all = pl.pallas_call(
        functools.partial(exp_body, nrow, tiles, chunk),
        grid=(tiles + 1,),
        in_specs=[
            pl.BlockSpec((tile, width), lambda t: (jnp.minimum(t, tiles - 1), 0)),
            pl.BlockSpec((cols, width), whole, pipeline_mode=once),
            pl.BlockSpec(pair_sum.shape, lambda t: (0, 0, 0), pipeline_mode=once),
            pl.BlockSpec(backward.shape, whole, pipeline_mode=once),
        ],
        out_specs=[
            pl.BlockSpec((tile, cols), behind),
            pl.BlockSpec((1, tile), beside),
            pl.BlockSpec((1, tile), beside),
            pl.BlockSpec(memory_space=pl.ANY),
        ],
        out_shape=[
            jax.ShapeDtypeStruct((rows, cols), BF16),
            jax.ShapeDtypeStruct((1, rows), F32),
            jax.ShapeDtypeStruct((1, rows), F32),
            jax.ShapeDtypeStruct((nrow, part, cols), BF16),
        ],
        scratch_shapes=[
            pltpu.VMEM((tile, cols), F32),
            pltpu.VMEM((tile, cols), F32),
            pltpu.VMEM((tile, 1), F32),
            pltpu.VMEM((tile, 1), F32),
            pltpu.VMEM((pairs, part, cols), BF16),
            pltpu.VMEM((part, cols), BF16),
        ]
        + [dma((pairs,))] * 6
        + [dma],
        compiler_params=pltpu.CompilerParams(
            dimension_semantics=("arbitrary",), collective_id=3, has_side_effects=True, vmem_limit_bytes=58 * MIB
        ),
        cost_estimate=pl.CostEstimate(
            flops=2 * rows * cols * width, bytes_accessed=200 * MIB, transcendentals=rows * cols
        ),
        name="exp_pass",
    )(src, tgt, pair_sum, backward)
    return exp_block, peak, sums, w_all.reshape(nrow * part, cols)


def reach_pass(exp_block, weighted):
    rows, cols = exp_block.shape
    seqs = weighted.shape[0]
    tile = fit(rows, 512)
    chunk = fit(cols, 2048)

    def body(w_ref, e_ref, reach_ref):
        total = jnp.zeros((tile, seqs), F32)
        for c in range(cols // chunk):
            at = pl.ds(c * chunk, chunk)
            total = total + lax.dot_general(e_ref[:, at], w_ref[:, at], NT, preferred_element_type=F32)
        reach_ref[...] = total.T

    return pl.pallas_call(
        body,
        grid=(rows // tile,),
        in_specs=[
            pl.BlockSpec((seqs, cols), lambda t: (0, 0), pipeline_mode=pl.Buffered(1)),
            pl.BlockSpec((tile, cols), lambda t: (t, 0)),
        ],
        out_specs=pl.BlockSpec((seqs, tile), lambda t: (0, t)),
        out_shape=jax.ShapeDtypeStruct((seqs, rows), F32),
        compiler_params=pltpu.CompilerParams(
            dimension_semantics=("arbitrary",), vmem_limit_bytes=58 * MIB
        ),
        cost_estimate=pl.CostEstimate(flops=2 * rows * cols * seqs, bytes_accessed=2 * rows * cols, transcendentals=0),
        name="reach_pass",
    )(weighted, exp_block)


def weights_body(nrow, ncol, factor, chunk, peak, sums, reach, fwd, coeffs, share,
                 stats, terms_col, terms_row, counts, rate, *sems):
    (a_s, a_r, b_s, b_r, c_s, c_r, d_s, d_r) = sems
    row, col = lax.axis_index("row"), lax.axis_index("col")
    cols = [(row, lax.rem(col + d, ncol)) for d in range(1, ncol)]
    rows = [(lax.rem(row + d, nrow), col) for d in range(1, nrow)]
    greet(cols + rows)
    size = reach.shape[1]

    def share_out(buffer, send, recv, devices):
        copies = [
            remote(buffer.at[0], buffer.at[d + 1], send.at[d], recv.at[d], to) for d, to in enumerate(devices)
        ]
        for copy in copies:
            copy.start()
        for copy in copies:
            copy.wait()

    stats[0, 0:1, :] = peak[...]
    stats[0, 1:2, :] = sums[...]
    share_out(stats, a_s, a_r, cols)
    best = stats[0, 0:1, :]
    for d in range(1, ncol):
        best = jnp.maximum(best, stats[d, 0:1, :])
    total = jnp.zeros_like(best)
    for d in range(ncol):
        total = total + stats[d, 1:2, :] * jnp.exp(stats[d, 0:1, :] - best)
    rate[0:1, :] = jnp.exp(peak[...] - best) / total

    def norm(c, carry):
        at = pl.ds(pl.multiple_of(c * chunk, chunk), chunk)
        term = fwd[:, at].astype(F32) * reach[:, at] * rate[0:1, at]
        return carry + jnp.sum(term, axis=1, keepdims=True)

    seqs = reach.shape[0]
    terms = lax.fori_loop(0, size // chunk, norm, jnp.zeros((seqs, 1), F32))
    terms_col[0] = to_row(terms)
    share_out(terms_col, b_s, b_r, cols)
    part = terms_col[0]
    for d in range(1, ncol):
        part = part + terms_col[d]
    terms_row[0] = part
    share_out(terms_row, c_s, c_r, rows)
    part = terms_row[0]
    for d in range(1, nrow):
        part = part + terms_row[d]
    inverse = to_column(factor / part)

    def weigh(c, carry):
        at = pl.ds(pl.multiple_of(c * chunk, chunk), chunk)
        made = (fwd[:, at].astype(F32) * inverse * rate[0:1, at]).astype(BF16)
        coeffs[:, at] = made
        counts[0, :, at] = jnp.sum(made.astype(F32) * reach[:, at], axis=0, keepdims=True)
        return carry

    lax.fori_loop(0, size // chunk, weigh, 0)
    share_out(counts, d_s, d_r, cols)
    count = counts[0]
    for d in range(1, ncol):
        count = count + counts[d]
    share[...] = count * rate[0:1, :]


def make_weights(nrow, ncol, factor, peak, sums, reach, forward):
    seqs, rows = reach.shape
    vmem = pl.BlockSpec(memory_space=pltpu.VMEM)
    dma = pltpu.SemaphoreType.DMA
    return pl.pallas_call(
        functools.partial(weights_body, nrow, ncol, factor, fit(rows, 512)),
        in_specs=[vmem] * 4,
        out_specs=[vmem] * 2,
        out_shape=[jax.ShapeDtypeStruct((seqs, rows), BF16), jax.ShapeDtypeStruct((1, rows), F32)],
        scratch_shapes=[
            pltpu.VMEM((ncol, 2, rows), F32),
            pltpu.VMEM((ncol, 1, seqs), F32),
            pltpu.VMEM((nrow, 1, seqs), F32),
            pltpu.VMEM((ncol, 1, rows), F32),
            pltpu.VMEM((1, rows), F32),
        ]
        + [dma((ncol - 1,))] * 4
        + [dma((nrow - 1,))] * 2
        + [dma((ncol - 1,))] * 2,
        compiler_params=pltpu.CompilerParams(
            collective_id=1, has_side_effects=True, vmem_limit_bytes=40 * MIB
        ),
        cost_estimate=pl.CostEstimate(flops=0, bytes_accessed=30 * MIB, transcendentals=0),
        name="make_weights",
    )(peak, sums, reach, forward)


def second_pass(exp_block, coeffs, share, weighted, tgt, src):
    rows, cols = exp_block.shape
    width = tgt.shape[1]
    seqs = weighted.shape[0]
    tile = fit(rows, 512)
    chunk = fit(cols, 1024)
    tiles = rows // tile
    turn = fit(cols, 1024)

    def body(e_ref, c_ref, share_ref, w_ref, tgt_ref, src_ref, gs_ref, gt_ref, total_ref):
        step = pl.program_id(0)

        @pl.when(step == 0)
        def _():
            total_ref[...] = jnp.zeros_like(total_ref)

        lead = c_ref[...].astype(F32).T.astype(BF16)
        flipped = src_ref[...].astype(F32).T.astype(BF16)
        level = to_column(share_ref[...])

        def make(c):
            at = pl.ds(c * chunk, chunk)
            summed = jnp.dot(lead, w_ref[:, at], preferred_element_type=F32)
            return (e_ref[:, at].astype(F32) * (summed - level)).astype(BF16)

        made = jnp.zeros((tile, width), F32)
        ahead = make(0)
        for c in range(cols // chunk):
            g = ahead
            if c + 1 < cols // chunk:
                ahead = make(c + 1)
            at = pl.ds(c * chunk, chunk)
            made = made + jnp.dot(g, tgt_ref[at, :], preferred_element_type=F32)
            total_ref[:, at] += jnp.dot(flipped, g, preferred_element_type=F32)
        gs_ref[...] = made.astype(BF16)

        @pl.when(step == tiles - 1)
        def _():
            def flip(c, carry):
                at = pl.ds(pl.multiple_of(c * turn, turn), turn)
                gt_ref[at, :] = total_ref[:, at].T.astype(BF16)
                return carry

            lax.fori_loop(0, cols // turn, flip, 0)

    once = pl.Buffered(1)
    by_row = lambda t: (t, 0)
    beside = lambda t: (0, t)
    whole = lambda t: (0, 0)
    return pl.pallas_call(
        body,
        grid=(tiles,),
        in_specs=[
            pl.BlockSpec((tile, cols), by_row),
            pl.BlockSpec((seqs, tile), beside),
            pl.BlockSpec((1, tile), beside),
            pl.BlockSpec((seqs, cols), whole, pipeline_mode=once),
            pl.BlockSpec((cols, width), whole, pipeline_mode=once),
            pl.BlockSpec((tile, width), by_row),
        ],
        out_specs=[
            pl.BlockSpec((tile, width), by_row),
            pl.BlockSpec((cols, width), whole, pipeline_mode=once),
        ],
        out_shape=[
            jax.ShapeDtypeStruct((rows, width), BF16),
            jax.ShapeDtypeStruct((cols, width), BF16),
        ],
        scratch_shapes=[pltpu.VMEM((width, cols), F32)],
        compiler_params=pltpu.CompilerParams(
            dimension_semantics=("arbitrary",), vmem_limit_bytes=58 * MIB
        ),
        cost_estimate=pl.CostEstimate(
            flops=2 * rows * cols * (2 * width + seqs), bytes_accessed=100 * MIB, transcendentals=0
        ),
        name="second_pass",
    )(exp_block, coeffs, share, weighted, tgt, src)


def scatter_body(nrow, ncol, ps, pt, out_src, out_tgt, col_in, pair_in, pair_out, chip_in, *sems):
    (a_s, a_r, b_s, b_r, c_s, c_r) = sems
    pairs = nrow // 2
    row, half, pair, sibling, across = row_peers(nrow)
    col = lax.axis_index("col")
    places = [lax.rem(col + d, ncol) for d in range(1, ncol)]
    greet([sibling] + across + [(row, place) for place in places])
    first = [remote(pt.at[2 * q + 1 - half], pair_in.at[q], b_s.at[q], b_r.at[q], sibling) for q in range(pairs)]
    for copy in first:
        copy.start()
    along = [
        remote(ps.at[place], col_in.at[d], a_s.at[d], a_r.at[d], (row, place)) for d, place in enumerate(places)
    ]
    for copy in along:
        copy.start()
    for copy in first:
        copy.wait()
    for d in range(1, pairs):
        q = lax.rem(pair + d, pairs)
        pair_out[d] = (pt[2 * q + half].astype(F32) + pair_in[q].astype(F32)).astype(BF16)
    second = [remote(pair_out.at[d], chip_in.at[d], c_s.at[d], c_r.at[d], across[d - 1]) for d in range(1, pairs)]
    for copy in second:
        copy.start()
    total = pt[2 * pair + half].astype(F32) + pair_in[pair].astype(F32)
    for d, copy in enumerate(second):
        copy.wait()
        total = total + chip_in[d + 1].astype(F32)
    out_tgt[...] = total
    total = ps[col].astype(F32)
    for d, copy in enumerate(along):
        copy.wait()
        total = total + col_in[d].astype(F32)
    out_src[...] = total


def scatter_sums(nrow, ncol, part_src, part_tgt):
    width = part_src.shape[1]
    src_rows = part_src.shape[0] // ncol
    tgt_rows = part_tgt.shape[0] // nrow
    pairs = nrow // 2
    vmem = pl.BlockSpec(memory_space=pltpu.VMEM)
    dma = pltpu.SemaphoreType.DMA
    return pl.pallas_call(
        functools.partial(scatter_body, nrow, ncol),
        in_specs=[vmem] * 2,
        out_specs=[vmem] * 2,
        out_shape=[
            jax.ShapeDtypeStruct((src_rows, width), F32),
            jax.ShapeDtypeStruct((tgt_rows, width), F32),
        ],
        scratch_shapes=[
            pltpu.VMEM((ncol - 1, src_rows, width), BF16),
            pltpu.VMEM((pairs, tgt_rows, width), BF16),
            pltpu.VMEM((pairs, tgt_rows, width), BF16),
            pltpu.VMEM((pairs, tgt_rows, width), BF16),
        ]
        + [dma((ncol - 1,))] * 2
        + [dma((pairs,))] * 4,
        compiler_params=pltpu.CompilerParams(
            collective_id=2, has_side_effects=True, vmem_limit_bytes=40 * MIB
        ),
        cost_estimate=pl.CostEstimate(flops=0, bytes_accessed=100 * MIB, transcendentals=0),
        name="scatter_sums",
    )(part_src.reshape(ncol, src_rows, width), part_tgt.reshape(nrow, tgt_rows, width))


def on_device(nrow, ncol, tokens, emission_table, forward_rows, backward_rows, src_embed, tgt_embed):
    src_block = lax.all_gather(src_embed, "col", axis=0, tiled=True)
    forward_all = lax.all_gather(forward_rows, "col", axis=0, tiled=True)
    vocab_local = emission_table.shape[0]
    offset = lax.axis_index("row") * vocab_local
    onehot = (tokens[:, None] == offset + jnp.arange(vocab_local, dtype=jnp.int32)[None, :]).astype(BF16)
    looked = jnp.dot(onehot, emission_table, preferred_element_type=F32).astype(BF16)
    tgt_block, pair_sum = gather_targets(nrow, looked, tgt_embed)
    exp_block, peak, sums, weighted = exp_pass(nrow, src_block, tgt_block, pair_sum, backward_rows)
    reach = reach_pass(exp_block, weighted)
    factor = forward_rows.shape[1] * nrow / tokens.shape[0]
    coeffs, share = make_weights(nrow, ncol, factor, peak, sums, reach, forward_all)
    part_src, part_tgt = second_pass(exp_block, coeffs, share, weighted, tgt_block, src_block)
    return scatter_sums(nrow, ncol, part_src, part_tgt)


def solution(mesh):
    in_specs = (
        P(),
        P("row", "col"),
        P("col", "row"),
        P("row", "col"),
        P(("row", "col"), None),
        P(("col", "row"), None),
    )
    out_specs = (P(("row", "col"), None), P(("col", "row"), None))
    return jax.shard_map(
        functools.partial(on_device, mesh.shape["row"], mesh.shape["col"]),
        mesh=mesh,
        in_specs=in_specs,
        out_specs=out_specs,
        check_vma=False,
    )
```
